32 devices in a mesh: ka: 2 (over core), slab: 16 (over z, y, x).
Axes of the slice: x: 2, y: 2, z: 4, core: 2. Of those that a mesh axis runs over, the one named last changes fastest.
Arguments:
- packet_prev: float32 [2, 128, 256, 384], P('ka', 'slab'), may hold values from -18 to 18
- packet_now: float32 [2, 128, 256, 384], P('ka', 'slab'), may hold values from -18 to 18
- potential: float32 [128, 256, 384], P('slab'), may hold values from 0.05 to 0.5
- kin_rho: float32 [128, 128], replicated, may hold values from -1 to 1, as said below
- kin_theta: float32 [256, 256], replicated, may hold values from -1 to 1, as said below
- kin_phi: float32 [384, 384], replicated, may hold values from -1 to 1, as said below
- damping: float32 [128], P('slab'), may hold values from 0.8 to 1
- inertia: float32 [128], P('slab'), may hold values from 0.05 to 0.3
- tilt: float32 [256], replicated, may hold values from 0.5 to 2
Outputs:
- packet_last: float32 [2, 128, 256, 384], P('ka', 'slab')
- packet_before: float32 [2, 128, 256, 384], P('ka', 'slab')
- intersections: float32 [2, 2], P(None, 'ka')
The draws below stay inside these ranges and needn't reach their ends.
Inputs may be any that keep to these rules, and one draw needn't show every extreme that they name: `kin_rho`: symmetric. `kin_theta`: symmetric. `kin_phi`: symmetric.
All inputs are finite; a program needn't handle non-finite values.
Results may differ from the reference program's by a relative error of at most 0.0001.
Values sent between devices are 32-bit elements; how exact they have to be, the bound alone decides.
A program may use at most 128 MiB of HBM per device.

```python
import math
import jax
import jax.numpy as jnp
from jax import lax

NR = 128
NT = 256
NP = 384
STEPS = 2
JTOT = 60
K_FIRST = 0
KBLOCKS = 2


def packet_field(key):
    radial = jnp.arange(NR).astype(jnp.float32) / float(NR - 1)
    values = jnp.clip(jax.random.normal(key, (KBLOCKS, NR, NT, NP), jnp.float32), -6.0, 6.0)
    scale = 1.0 + 2.0 * radial
    return values * scale[None, :, None, None]


def draw_packet_prev(key, part):
    return packet_field(jax.random.fold_in(key, 11))


def draw_packet_now(key, part):
    return packet_field(jax.random.fold_in(key, 23))


def kinetic_matrix(key, order):
    base = jnp.clip(jax.random.normal(key, (order, order), jnp.float32), -4.0, 4.0)
    return (base + base.T) * (0.085 / float(order) ** 0.5)


def draw_kin_rho(key, part):
    return kinetic_matrix(jax.random.fold_in(key, 31), NR)


def draw_kin_theta(key, part):
    return kinetic_matrix(jax.random.fold_in(key, 37), NT)


def draw_kin_phi(key, part):
    return kinetic_matrix(jax.random.fold_in(key, 41), NP)


def level_of(rng, shape, pieces, low, largest):
    factor_of = 1.0
    for dim, parts in pieces:
        heights = jax.random.uniform(jax.random.fold_in(jax.random.fold_in(rng, 6), dim), (parts,), jnp.float32, low / len(pieces), largest / len(pieces))
        factor_of = factor_of * jnp.repeat(jnp.exp(heights), shape[dim] // parts).reshape((-1,) + (1,) * (len(shape) - 1 - dim))
    return factor_of


def setup_inputs(seed: int = 0) -> dict:
    keys = jax.random.split(jax.random.key(seed), 10)
    return {
        "packet_prev": draw_packet_prev(jax.random.fold_in(keys[9], 71), 0),
        "packet_now": draw_packet_now(jax.random.fold_in(keys[9], 71), 0),
        "potential": jnp.clip(0.05 + 0.45 * jax.random.uniform(keys[2], (NR, NT, NP), jnp.float32) ** level_of(keys[2], (NR, NT, NP), ((0, 16),), -0.2, 0.2), 0.05, 0.5),
        "kin_rho": draw_kin_rho(jax.random.fold_in(keys[9], 71), 0),
        "kin_theta": draw_kin_theta(jax.random.fold_in(keys[9], 71), 0),
        "kin_phi": draw_kin_phi(jax.random.fold_in(keys[9], 71), 0),
        "damping": jnp.clip(0.8 + 0.19999999 * jax.random.uniform(keys[6], (NR,), jnp.float32) ** level_of(keys[6], (NR,), ((0, 16),), -0.2, 0.2), 0.8, 1.0),
        "inertia": jnp.clip(jnp.exp(math.log(0.3) - 1.7917595 * jax.random.uniform(keys[7], (NR,), jnp.float32) ** level_of(keys[7], (NR,), ((0, 16),), -0.2, 0.2)), 0.05, 0.3),
        "tilt": jnp.clip(jax.random.uniform(keys[8], (NT,), jnp.float32, 0.5, 2.0), 0.5, 2.0),
    }


HI = lax.Precision.HIGHEST

def apply_h(q, potential, kin_rho, kin_theta, kin_phi, inertia, tilt):
    kvals = (K_FIRST + jnp.arange(KBLOCKS)).astype(jnp.float32)
    jj = float(JTOT * (JTOT + 1))
    cent = (jj - 2.0 * kvals * kvals) / float(JTOT * JTOT)
    lam = jnp.sqrt(jj - kvals * (kvals + 1.0)) / float(JTOT)
    rho_part = jnp.einsum('sr,krtp->kstp', kin_rho, q, precision=HI)
    theta_part = jnp.einsum('ts,krsp->krtp', kin_theta, q, precision=HI)
    phi_part = jnp.einsum('krts,sp->krtp', q, kin_phi, precision=HI)
    zero_block = jnp.zeros_like(q[:1])
    above = jnp.concatenate([q[1:], zero_block], axis=0) * lam[:, None, None, None]
    lam_below = jnp.concatenate([jnp.zeros((1,), jnp.float32), lam[:-1]])
    below = jnp.concatenate([zero_block, q[:-1]], axis=0) * lam_below[:, None, None, None]
    coupling = inertia[None, :, None, None] * tilt[None, None, :, None] * (above + below)
    diag = potential[None] + inertia[None, :, None, None] * cent[:, None, None, None]
    return rho_part + theta_part + phi_part + diag * q + coupling

def reference(packet_prev, packet_now, potential, kin_rho, kin_theta, kin_phi, damping, inertia, tilt):
    q_prev = packet_prev
    q = packet_now
    damp = damping[None, :, None, None]
    intersection_list = []
    for step in range(STEPS):
        image = apply_h(q, potential, kin_rho, kin_theta, kin_phi, inertia, tilt)
        q_new = damp * (2.0 * image - damp * q_prev)
        intersection_list.append(lax.optimization_barrier(jnp.mean(packet_now * q_new, axis=(1, 2, 3))))
        q_prev = q
        q = q_new
    return (q, q_prev, jnp.stack(intersection_list, axis=0))
```

```python
import functools

import jax
import jax.numpy as jnp
from jax import lax
from jax.experimental import pallas as pl
from jax.experimental.pallas import tpu as pltpu
from jax.sharding import PartitionSpec as P

NR = 128
NT = 256
NP = 384
STEPS = 2
JTOT = 60
K_FIRST = 0


HI = lax.Precision.HIGHEST


def padded(cells, sides, width):
    for axis, dim in sides:
        count = lax.axis_size(axis)
        ends = count - 1
        head = lax.slice_in_dim(cells, 0, width, axis=dim)
        tail = lax.slice_in_dim(cells, cells.shape[dim] - width, cells.shape[dim], axis=dim)
        cells = jnp.concatenate(
            [
                lax.ppermute(tail, axis, [(i, (i + 1) % count) for i in range(ends)]),
                cells,
                lax.ppermute(head, axis, [((i + 1) % count, i) for i in range(ends)]),
            ],
            axis=dim,
        )
    return cells


def rho_apply(kin_rho, whole):
    return jnp.einsum("sr,rtp->stp", kin_rho, whole, precision=HI)


def apply_h(q, potential, kin_rho, kin_theta, kin_phi, inertia, tilt):
    kval = (K_FIRST + lax.axis_index("ka")).astype(jnp.float32)
    jj = float(JTOT * (JTOT + 1))
    cent = (jj - 2.0 * kval * kval) / float(JTOT * JTOT)
    lam_here = jnp.sqrt(jj - kval * (kval + 1.0)) / float(JTOT)
    lam_below = jnp.sqrt(jj - (kval - 1.0) * kval) / float(JTOT)
    near = padded(q, (("ka", 0),), 1)
    field = q[0]
    term = rho_apply(
        kin_rho, lax.all_to_all(field, "slab", split_axis=1, concat_axis=0, tiled=True)
    )
    rho_part = lax.all_to_all(term, "slab", split_axis=0, concat_axis=1, tiled=True)
    theta_part = jnp.einsum("ts,rsp->rtp", kin_theta, field, precision=HI)
    rows = field.shape[0] * field.shape[1]
    phi_part = jnp.dot(field.reshape(rows, field.shape[2]), kin_phi, precision=HI).reshape(
        field.shape
    )
    coupling = (
        inertia[:, None, None] * tilt[None, :, None] * (lam_here * near[2] + lam_below * near[0])
    )
    diag = potential + inertia[:, None, None] * cent
    total = rho_part + theta_part + phi_part + diag * field + coupling
    return total[None]


def shards(packet_prev, packet_now, potential, kin_rho, kin_theta, kin_phi, damping, inertia, tilt):
    damp = damping[None, :, None, None]
    cells = float(NR * NT * NP)
    q_prev = packet_prev
    q = packet_now
    partials = []
    for step in range(STEPS):
        image = apply_h(q, potential, kin_rho, kin_theta, kin_phi, inertia, tilt)
        q_new = damp * (2.0 * image - damp * q_prev)
        local_sum = jnp.sum(packet_now * q_new, axis=(1, 2, 3))
        partials.append(lax.psum(local_sum, "slab") / cells)
        q_prev = q
        q = q_new
    intersections = jnp.stack(partials, axis=0)
    return (q, q_prev, intersections)


MESH = pl.DeviceIdType.MESH
Q0, P1, U, V = range(4)


def split(x):
    high = x.astype(jnp.bfloat16)
    return high, (x - high.astype(jnp.float32)).astype(jnp.bfloat16)


def dot3(a, b):
    dot = functools.partial(jnp.dot, preferred_element_type=jnp.float32)
    return dot(a[0], b[0]) + (dot(a[0], b[1]) + dot(a[1], b[0]))


def partner(me, d, n):
    out = 0
    bit = 1
    while bit < n:
        out = out + ((me // bit + d // bit) % 2) * bit
        bit *= 2
    return out


def fused(
    n, q_in, prev_in, pot_in, rho_in, theta_in, phi_in, damp, inertia, tilt,
    last_out, before_out, stat_out,
    q0, prev, pot, near0, qb, p1, pb, ub, ua, vb, va, q1, near1, w, qx, ux,
    rho_hi, rho_lo, theta_hi, theta_lo, phi_hi, phi_lo, dmine, dall, stat_mine, stat_all,
    load_sem, out_sem, own_sem, ka_send, ka_recv, send, recv, small_send, small_recv,
):
    rows, nt, width = q0.shape
    cols = qb.shape[1]
    me = lax.axis_index("slab")
    ka = lax.axis_index("ka")
    peers = list(range(1, n))

    loads = [
        pltpu.make_async_copy(q_in, q0, load_sem.at[0]),
        pltpu.make_async_copy(prev_in, prev, load_sem.at[1]),
        pltpu.make_async_copy(pot_in, pot, load_sem.at[2]),
    ]
    for load in loads:
        load.start()

    barrier = pltpu.get_barrier_semaphore()
    for d in peers:
        pl.semaphore_signal(
            barrier, inc=1, device_id={"slab": partner(me, d, n)}, device_id_type=MESH
        )
    pl.semaphore_signal(barrier, inc=1, device_id={"ka": 1 - ka}, device_id_type=MESH)
    pl.semaphore_wait(barrier, n)

    def tees(j):
        return pl.ds(pl.multiple_of(j * cols, cols), cols)

    def rhos(j):
        return pl.ds(pl.multiple_of(j * rows, rows), rows)

    def away(phase, d, src, dst):
        there = partner(me, d, n)
        return pltpu.make_async_remote_copy(
            src_ref=src.at[:, tees(there), :],
            dst_ref=dst.at[rhos(me)],
            send_sem=send.at[phase, d],
            recv_sem=recv.at[phase, d],
            device_id={"slab": there},
            device_id_type=MESH,
        )

    def away_arrival(phase, d, src, dst):
        there = partner(me, d, n)
        return pltpu.make_async_remote_copy(
            src_ref=src.at[:, tees(there), :],
            dst_ref=dst.at[rhos(there)],
            send_sem=send.at[phase, d],
            recv_sem=recv.at[phase, d],
            device_id={"slab": there},
            device_id_type=MESH,
        )

    def back(phase, d, src, dst):
        there = partner(me, d, n)
        return pltpu.make_async_remote_copy(
            src_ref=src.at[rhos(there)],
            dst_ref=dst.at[:, tees(me), :],
            send_sem=send.at[phase, d],
            recv_sem=recv.at[phase, d],
            device_id={"slab": there},
            device_id_type=MESH,
        )

    def back_arrival(phase, d, src, dst):
        there = partner(me, d, n)
        return pltpu.make_async_remote_copy(
            src_ref=src.at[rhos(there)],
            dst_ref=dst.at[:, tees(there), :],
            send_sem=send.at[phase, d],
            recv_sem=recv.at[phase, d],
            device_id={"slab": there},
            device_id_type=MESH,
        )

    def across(k, src, dst):
        return pltpu.make_async_remote_copy(
            src_ref=src,
            dst_ref=dst,
            send_sem=ka_send.at[k],
            recv_sem=ka_recv.at[k],
            device_id={"ka": 1 - ka},
            device_id_type=MESH,
        )

    def small(k, d, src, dst, slot):
        there = partner(me, d, n)
        return pltpu.make_async_remote_copy(
            src_ref=src,
            dst_ref=dst.at[slot],
            send_sem=small_send.at[k, d],
            recv_sem=small_recv.at[k, d],
            device_id={"slab": there},
            device_id_type=MESH,
        )

    across(0, q_in, near0).start()
    for d in peers:
        away(Q0, d, q_in, qb).start()
    own_q = pltpu.make_async_copy(q_in.at[:, tees(me), :], qb.at[rhos(me)], own_sem.at[Q0])
    own_q.start()

    for r in range(rows):
        dmine[r : r + 1, :] = jnp.full((1, dmine.shape[1]), damp[r], jnp.float32)
    for d in peers:
        small(0, d, dmine, dall, me).start()
    dall[me] = dmine[...]

    for ref, high, low in (
        (rho_in, rho_hi, rho_lo), (theta_in, theta_hi, theta_lo), (phi_in, phi_hi, phi_lo)
    ):
        high[...], low[...] = split(ref[...])

    kval = (K_FIRST + ka).astype(jnp.float32)
    kmin = float(K_FIRST)
    jj = float(JTOT * (JTOT + 1))
    cent = (jj - 2.0 * kval * kval) / float(JTOT * JTOT)
    lam = ((jj - kmin * (kmin + 1.0)) ** 0.5) / float(JTOT)

    def image(field, near, r):
        x = field[r]
        parts = split(x)
        total = dot3((theta_hi[...], theta_lo[...]), parts)
        total += dot3(parts, (phi_hi[...], phi_lo[...]))
        total += (pot[r] + inertia[r] * cent) * x
        slope = (inertia[r] * lam) * tilt[...]
        return total + jnp.concatenate([slope] * (width // 128), axis=1) * near[r]

    for load in loads:
        load.wait()
    across(0, q_in, near0).wait()

    @pl.loop(0, rows)
    def _(r):
        p1[r] = damp[r] * (2.0 * image(q0, near0, r) - damp[r] * prev[r])

    for d in peers:
        away(Q0, d, q_in, qb).wait_send()
        away(P1, d, p1, pb).start()
    own_p = pltpu.make_async_copy(p1.at[:, tees(me), :], pb.at[rhos(me)], own_sem.at[P1])
    own_p.start()
    for d in peers:
        away_arrival(Q0, d, q_in, qb).wait_recv()
    own_q.wait()

    chunks = [(b, c) for b in range(cols // 8) for c in range(width // 128)]
    full = n * rows

    def wide(ref, b, c):
        return ref[:, 8 * b : 8 * b + 8, 128 * c : 128 * c + 128].reshape(full, 1024)

    def narrow(ref, b, c, value):
        ref[:, 8 * b : 8 * b + 8, 128 * c : 128 * c + 128] = value.reshape(full, 8, 128)

    for i, (b, c) in enumerate(chunks):
        x = wide(qb, b, c)
        qx[i] = x
        u = dot3((rho_hi[...], rho_lo[...]), split(x))
        ux[i] = u
        narrow(ub, b, c, u)

    for d in peers:
        away(P1, d, p1, pb).wait_send()
        back(U, d, ub, ua).start()
    own_u = pltpu.make_async_copy(ub.at[rhos(me)], ua.at[:, tees(me), :], own_sem.at[U])
    own_u.start()
    for d in peers:
        away_arrival(P1, d, p1, pb).wait_recv()
        small(0, d, dmine, dall, partner(me, d, n)).wait_recv()
    own_p.wait()

    dcol = 2.0 * dall[...].reshape(full, 128)
    dwide = jnp.concatenate([dcol] * 8, axis=1)
    acc2 = jnp.zeros((8, 128), jnp.float32)
    for i, (b, c) in enumerate(chunks):
        x = wide(pb, b, c) + dwide * ux[i]
        v = dot3((rho_hi[...], rho_lo[...]), split(x))
        narrow(vb, b, c, v)
        prod = (qx[i] * v) * dwide
        part = jnp.sum(prod.reshape(full // 8, 8, 1024), axis=0)
        for k in range(8):
            acc2 += part[:, 128 * k : 128 * k + 128]
    stat_mine[8:16, :] = acc2

    for d in peers:
        back(U, d, ub, ua).wait_send()
        back(V, d, vb, va).start()
    own_v = pltpu.make_async_copy(vb.at[rhos(me)], va.at[:, tees(me), :], own_sem.at[V])
    own_v.start()
    for d in peers:
        back_arrival(U, d, ub, ua).wait_recv()
    own_u.wait()

    def gather(prod):
        part = jnp.sum(prod.reshape(nt // 8, 8, width), axis=0)
        out = part[:, :128]
        for k in range(1, width // 128):
            out += part[:, 128 * k : 128 * k + 128]
        return out

    stat_mine[0:8, :] = jnp.zeros((8, 128), jnp.float32)

    @pl.loop(0, rows)
    def _(r):
        new = p1[r] + (2.0 * damp[r]) * ua[r]
        q1[r] = new
        stat_mine[0:8, :] += gather(q0[r] * new)

    across(1, q1, near1).start()
    before = pltpu.make_async_copy(q1, before_out, out_sem.at[0])
    before.start()
    across(1, q1, near1).wait()

    @pl.loop(0, rows)
    def _(r):
        new = damp[r] * (2.0 * image(q1, near1, r) - damp[r] * q0[r])
        w[r] = new
        stat_mine[8:16, :] += gather(q0[r] * new)

    for d in peers:
        small(1, d, stat_mine, stat_all, me).start()
    stat_all[me] = stat_mine[...]

    def finish(j, k):
        for r in range(rows):
            w[r, tees(j), :] += (2.0 * damp[r]) * va[r, tees(j), :]
        pltpu.make_async_copy(
            w.at[:, tees(j), :], last_out.at[:, tees(j), :], out_sem.at[1 + k]
        ).start()

    own_v.wait()
    finish(me, 0)
    for d in peers:
        back_arrival(V, d, vb, va).wait_recv()
        finish(partner(me, d, n), d)

    for d in peers:
        small(1, d, stat_mine, stat_all, partner(me, d, n)).wait_recv()
    total = jnp.sum(stat_all[...], axis=0)
    scale = 1.0 / float(NR * NT * NP)
    stat_out[0:1, :] = jnp.full((1, 128), jnp.sum(total[0:8, :]) * scale, jnp.float32)
    stat_out[1:2, :] = jnp.full((1, 128), jnp.sum(total[8:16, :]) * scale, jnp.float32)

    for d in peers:
        back(V, d, vb, va).wait_send()
        small(0, d, dmine, dall, me).wait_send()
        small(1, d, stat_mine, stat_all, me).wait_send()
    before.wait()
    for k, j in [(0, me)] + [(d, partner(me, d, n)) for d in peers]:
        pltpu.make_async_copy(
            w.at[:, tees(j), :], last_out.at[:, tees(j), :], out_sem.at[1 + k]
        ).wait()


def fused_shards(
    packet_prev, packet_now, potential, kin_rho, kin_theta, kin_phi, damping, inertia, tilt
):
    n = lax.axis_size("slab")
    _, rows, nt, width = packet_now.shape
    cols, full = nt // n, n * rows
    slab = pltpu.VMEM((rows, nt, width), jnp.float32)
    turned = pltpu.VMEM((full, cols, width), jnp.float32)
    pieces = (cols // 8) * (width // 128)
    flat = pltpu.VMEM((pieces, full, 1024), jnp.float32)

    def half(order):
        return [pltpu.VMEM((order, order), jnp.bfloat16)] * 2

    hbm = pl.BlockSpec(memory_space=pl.ANY)
    vmem = pl.BlockSpec(memory_space=pltpu.VMEM)
    smem = pl.BlockSpec(memory_space=pltpu.SMEM)
    dma = pltpu.SemaphoreType.DMA
    field = jax.ShapeDtypeStruct((rows, nt, width), jnp.float32)
    last, before, stats = pl.pallas_call(
        functools.partial(fused, n),
        out_shape=(field, field, jax.ShapeDtypeStruct((2, 128), jnp.float32)),
        in_specs=[hbm] * 3 + [vmem] * 3 + [smem] * 2 + [vmem],
        out_specs=(hbm, hbm, vmem),
        scratch_shapes=[
            slab, slab, slab, slab, turned, slab, turned, turned, slab, turned, slab,
            slab, slab, slab, flat, flat,
            *half(full), *half(nt), *half(width),
            pltpu.VMEM((rows, 128), jnp.float32),
            pltpu.VMEM((n, rows, 128), jnp.float32),
            pltpu.VMEM((16, 128), jnp.float32),
            pltpu.VMEM((n, 16, 128), jnp.float32),
            dma((3,)), dma((n + 1,)), dma((4,)), dma((2,)), dma((2,)),
            dma((4, n)), dma((4, n)), dma((2, n)), dma((2, n)),
        ],
        compiler_params=pltpu.CompilerParams(
            collective_id=0, has_side_effects=True, vmem_limit_bytes=60 * 2**20
        ),
        name="chebyshev",
    )(
        packet_now[0], packet_prev[0], potential, kin_rho, kin_theta, kin_phi, damping, inertia,
        jnp.broadcast_to(tilt[:, None], (nt, 128)),
    )
    return last[None], before[None], stats[:, :1]


def fits_fused(mesh):
    n = mesh.shape["slab"]
    return (
        mesh.shape["ka"] == 2
        and STEPS == 2
        and n > 1
        and n & (n - 1) == 0
        and NR == 8 * n
        and NT % (8 * n) == 0
        and NP % 128 == 0
    )


def solution(mesh):
    return jax.shard_map(
        fused_shards if fits_fused(mesh) else shards,
        mesh=mesh,
        in_specs=(
            P("ka", "slab", None, None),
            P("ka", "slab", None, None),
            P("slab", None, None),
            P(),
            P(),
            P(),
            P("slab"),
            P("slab"),
            P(),
        ),
        out_specs=(P("ka", "slab", None, None), P("ka", "slab", None, None), P(None, "ka")),
        check_vma=False,
    )
```

```python
import functools

import jax
import jax.numpy as jnp
from jax import lax
from jax.experimental import pallas as pl
from jax.experimental.pallas import tpu as pltpu
from jax.sharding import PartitionSpec as P

NR = 128
NT = 256
NP = 384
STEPS = 2
JTOT = 60
K_FIRST = 0


HI = lax.Precision.HIGHEST


def padded(cells, sides, width):
    for axis, dim in sides:
        count = lax.axis_size(axis)
        ends = count - 1
        head = lax.slice_in_dim(cells, 0, width, axis=dim)
        tail = lax.slice_in_dim(cells, cells.shape[dim] - width, cells.shape[dim], axis=dim)
        cells = jnp.concatenate(
            [
                lax.ppermute(tail, axis, [(i, (i + 1) % count) for i in range(ends)]),
                cells,
                lax.ppermute(head, axis, [((i + 1) % count, i) for i in range(ends)]),
            ],
            axis=dim,
        )
    return cells


def rho_apply(kin_rho, whole):
    return jnp.einsum("sr,rtp->stp", kin_rho, whole, precision=HI)


def apply_h(q, potential, kin_rho, kin_theta, kin_phi, inertia, tilt):
    kval = (K_FIRST + lax.axis_index("ka")).astype(jnp.float32)
    jj = float(JTOT * (JTOT + 1))
    cent = (jj - 2.0 * kval * kval) / float(JTOT * JTOT)
    lam_here = jnp.sqrt(jj - kval * (kval + 1.0)) / float(JTOT)
    lam_below = jnp.sqrt(jj - (kval - 1.0) * kval) / float(JTOT)
    near = padded(q, (("ka", 0),), 1)
    field = q[0]
    term = rho_apply(
        kin_rho, lax.all_to_all(field, "slab", split_axis=1, concat_axis=0, tiled=True)
    )
    rho_part = lax.all_to_all(term, "slab", split_axis=0, concat_axis=1, tiled=True)
    theta_part = jnp.einsum("ts,rsp->rtp", kin_theta, field, precision=HI)
    rows = field.shape[0] * field.shape[1]
    phi_part = jnp.dot(field.reshape(rows, field.shape[2]), kin_phi, precision=HI).reshape(
        field.shape
    )
    coupling = (
        inertia[:, None, None] * tilt[None, :, None] * (lam_here * near[2] + lam_below * near[0])
    )
    diag = potential + inertia[:, None, None] * cent
    total = rho_part + theta_part + phi_part + diag * field + coupling
    return total[None]


def shards(packet_prev, packet_now, potential, kin_rho, kin_theta, kin_phi, damping, inertia, tilt):
    damp = damping[None, :, None, None]
    cells = float(NR * NT * NP)
    q_prev = packet_prev
    q = packet_now
    partials = []
    for step in range(STEPS):
        image = apply_h(q, potential, kin_rho, kin_theta, kin_phi, inertia, tilt)
        q_new = damp * (2.0 * image - damp * q_prev)
        local_sum = jnp.sum(packet_now * q_new, axis=(1, 2, 3))
        partials.append(lax.psum(local_sum, "slab") / cells)
        q_prev = q
        q = q_new
    intersections = jnp.stack(partials, axis=0)
    return (q, q_prev, intersections)


MESH = pl.DeviceIdType.MESH
Q0, P1, U, V = range(4)


def split(x):
    high = x.astype(jnp.bfloat16)
    return high, (x - high.astype(jnp.float32)).astype(jnp.bfloat16)


def dot3(a, b):
    dot = functools.partial(jnp.dot, preferred_element_type=jnp.float32)
    return dot(a[0], b[0]) + (dot(a[0], b[1]) + dot(a[1], b[0]))


def partner(me, d, n):
    out = 0
    bit = 1
    while bit < n:
        out = out + ((me // bit + d // bit) % 2) * bit
        bit *= 2
    return out


def fused(
    n, q_in, prev_in, pot_in, rho_in, theta_in, phi_in, damp_in, inertia_in, tilt_in,
    last_out, before_out, stat_out,
    q0, prev, pot, near0, qb, p1, pb, ub, ua, vb, va, near1, qx, ux, slope,
    rho, theta, phi, damp, inertia, tilt,
    rho_hi, rho_lo, theta_hi, theta_lo, phi_hi, phi_lo, dmine, dall, stat_mine, stat_all,
    load_sem, out_sem, own_sem, ka_send, ka_recv, send, recv, small_send, small_recv,
):
    rows, nt, width = q0.shape
    cols = qb.shape[1]
    me = lax.axis_index("slab")
    ka = lax.axis_index("ka")
    peers = list(range(1, n))

    loads = [
        pltpu.make_async_copy(q_in, q0, load_sem.at[0]),
        pltpu.make_async_copy(prev_in, prev, load_sem.at[1]),
        pltpu.make_async_copy(pot_in, pot, load_sem.at[2]),
        pltpu.make_async_copy(rho_in, rho, load_sem.at[3]),
        pltpu.make_async_copy(theta_in, theta, load_sem.at[4]),
        pltpu.make_async_copy(phi_in, phi, load_sem.at[5]),
        pltpu.make_async_copy(damp_in, damp, load_sem.at[6]),
        pltpu.make_async_copy(inertia_in, inertia, load_sem.at[7]),
        pltpu.make_async_copy(tilt_in, tilt, load_sem.at[8]),
    ]
    for load in loads:
        load.start()

    barrier = pltpu.get_barrier_semaphore()
    for d in peers:
        pl.semaphore_signal(
            barrier, inc=1, device_id={"slab": partner(me, d, n)}, device_id_type=MESH
        )
    pl.semaphore_signal(barrier, inc=1, device_id={"ka": 1 - ka}, device_id_type=MESH)
    pl.semaphore_wait(barrier, n)

    def tees(j):
        return pl.ds(pl.multiple_of(j * cols, cols), cols)

    def rhos(j):
        return pl.ds(pl.multiple_of(j * rows, rows), rows)

    def away(phase, d, src, dst):
        there = partner(me, d, n)
        return pltpu.make_async_remote_copy(
            src_ref=src.at[:, tees(there), :],
            dst_ref=dst.at[rhos(me)],
            send_sem=send.at[phase, d],
            recv_sem=recv.at[phase, d],
            device_id={"slab": there},
            device_id_type=MESH,
        )

    def away_arrival(phase, d, src, dst):
        there = partner(me, d, n)
        return pltpu.make_async_remote_copy(
            src_ref=src.at[:, tees(there), :],
            dst_ref=dst.at[rhos(there)],
            send_sem=send.at[phase, d],
            recv_sem=recv.at[phase, d],
            device_id={"slab": there},
            device_id_type=MESH,
        )

    def back(phase, d, src, dst):
        there = partner(me, d, n)
        return pltpu.make_async_remote_copy(
            src_ref=src.at[rhos(there)],
            dst_ref=dst.at[:, tees(me), :],
            send_sem=send.at[phase, d],
            recv_sem=recv.at[phase, d],
            device_id={"slab": there},
            device_id_type=MESH,
        )

    def back_arrival(phase, d, src, dst):
        there = partner(me, d, n)
        return pltpu.make_async_remote_copy(
            src_ref=src.at[rhos(there)],
            dst_ref=dst.at[:, tees(there), :],
            send_sem=send.at[phase, d],
            recv_sem=recv.at[phase, d],
            device_id={"slab": there},
            device_id_type=MESH,
        )

    def across(k, src, dst):
        return pltpu.make_async_remote_copy(
            src_ref=src,
            dst_ref=dst,
            send_sem=ka_send.at[k],
            recv_sem=ka_recv.at[k],
            device_id={"ka": 1 - ka},
            device_id_type=MESH,
        )

    def small(k, d, src, dst, slot):
        there = partner(me, d, n)
        return pltpu.make_async_remote_copy(
            src_ref=src,
            dst_ref=dst.at[slot],
            send_sem=small_send.at[k, d],
            recv_sem=small_recv.at[k, d],
            device_id={"slab": there},
            device_id_type=MESH,
        )

    across(0, q_in, near0).start()
    for d in peers:
        away(Q0, d, q_in, qb).start()
    own_q = pltpu.make_async_copy(q_in.at[:, tees(me), :], qb.at[rhos(me)], own_sem.at[Q0])
    own_q.start()

    for load in loads:
        load.wait()
    for r in range(rows):
        dmine[r : r + 1, :] = jnp.full((1, dmine.shape[1]), damp[r], jnp.float32)
    for d in peers:
        small(0, d, dmine, dall, me).start()
    dall[me] = dmine[...]

    @pl.loop(0, nt // 8)
    def _(i):
        at = pl.ds(pl.multiple_of(8 * i, 8), 8)
        slope[at, :] = jnp.concatenate(
            [jnp.full((1, 128), tilt[8 * i + k], jnp.float32) for k in range(8)], axis=0
        )

    for ref, high, low in (
        (rho, rho_hi, rho_lo), (theta, theta_hi, theta_lo), (phi, phi_hi, phi_lo)
    ):
        high[...], low[...] = split(ref[...])

    kval = (K_FIRST + ka).astype(jnp.float32)
    kmin = float(K_FIRST)
    jj = float(JTOT * (JTOT + 1))
    cent = (jj - 2.0 * kval * kval) / float(JTOT * JTOT)
    lam = ((jj - kmin * (kmin + 1.0)) ** 0.5) / float(JTOT)

    def image(field, near, r):
        x = field[r]
        parts = split(x)
        total = dot3((theta_hi[...], theta_lo[...]), parts)
        total += dot3(parts, (phi_hi[...], phi_lo[...]))
        total += (pot[r] + inertia[r] * cent) * x
        tilted = (inertia[r] * lam) * slope[...]
        return total + jnp.concatenate([tilted] * (width // 128), axis=1) * near[r]

    across(0, q_in, near0).wait()

    @pl.loop(0, rows)
    def _(r):
        p1[r] = damp[r] * (2.0 * image(q0, near0, r) - damp[r] * prev[r])

    for d in peers:
        away(Q0, d, q_in, qb).wait_send()
        away(P1, d, p1, pb).start()
    own_p = pltpu.make_async_copy(p1.at[:, tees(me), :], pb.at[rhos(me)], own_sem.at[P1])
    own_p.start()
    for d in peers:
        away_arrival(Q0, d, q_in, qb).wait_recv()
    own_q.wait()

    chunks = [(b, c) for b in range(cols // 8) for c in range(width // 128)]
    full = n * rows

    def wide(ref, b, c):
        return ref[:, 8 * b : 8 * b + 8, 128 * c : 128 * c + 128].reshape(full, 1024)

    def narrow(ref, b, c, value):
        ref[:, 8 * b : 8 * b + 8, 128 * c : 128 * c + 128] = value.reshape(full, 8, 128)

    for i, (b, c) in enumerate(chunks):
        x = wide(qb, b, c)
        qx[i] = x
        u = dot3((rho_hi[...], rho_lo[...]), split(x))
        ux[i] = u
        narrow(ub, b, c, u)

    for d in peers:
        away(P1, d, p1, pb).wait_send()
        back(U, d, ub, ua).start()
    own_u = pltpu.make_async_copy(ub.at[rhos(me)], ua.at[:, tees(me), :], own_sem.at[U])
    own_u.start()
    for d in peers:
        away_arrival(P1, d, p1, pb).wait_recv()
        small(0, d, dmine, dall, partner(me, d, n)).wait_recv()
    own_p.wait()

    dcol = 2.0 * dall[...].reshape(full, 128)
    dwide = jnp.concatenate([dcol] * 8, axis=1)
    acc2 = jnp.zeros((8, 128), jnp.float32)
    for i, (b, c) in enumerate(chunks):
        x = wide(pb, b, c) + dwide * ux[i]
        v = dot3((rho_hi[...], rho_lo[...]), split(x))
        narrow(vb, b, c, v)
        prod = (qx[i] * v) * dwide
        part = jnp.sum(prod.reshape(full // 8, 8, 1024), axis=0)
        for k in range(8):
            acc2 += part[:, 128 * k : 128 * k + 128]
    stat_mine[8:16, :] = acc2

    for d in peers:
        back(U, d, ub, ua).wait_send()
        back(V, d, vb, va).start()
    own_v = pltpu.make_async_copy(vb.at[rhos(me)], va.at[:, tees(me), :], own_sem.at[V])
    own_v.start()
    for d in peers:
        back_arrival(U, d, ub, ua).wait_recv()
    own_u.wait()

    def gather(prod):
        part = jnp.sum(prod.reshape(nt // 8, 8, width), axis=0)
        out = part[:, :128]
        for k in range(1, width // 128):
            out += part[:, 128 * k : 128 * k + 128]
        return out

    stat_mine[0:8, :] = jnp.zeros((8, 128), jnp.float32)

    @pl.loop(0, rows)
    def _(r):
        new = p1[r] + (2.0 * damp[r]) * ua[r]
        p1[r] = new
        stat_mine[0:8, :] += gather(q0[r] * new)

    across(1, p1, near1).start()
    before = pltpu.make_async_copy(p1, before_out, out_sem.at[0])
    before.start()
    across(1, p1, near1).wait()

    @pl.loop(0, rows)
    def _(r):
        new = damp[r] * (2.0 * image(p1, near1, r) - damp[r] * q0[r])
        prev[r] = new
        stat_mine[8:16, :] += gather(q0[r] * new)

    for d in peers:
        small(1, d, stat_mine, stat_all, me).start()
    stat_all[me] = stat_mine[...]

    def finish(j, k):
        for r in range(rows):
            prev[r, tees(j), :] += (2.0 * damp[r]) * va[r, tees(j), :]
        pltpu.make_async_copy(
            prev.at[:, tees(j), :], last_out.at[:, tees(j), :], out_sem.at[1 + k]
        ).start()

    own_v.wait()
    finish(me, 0)
    for d in peers:
        back_arrival(V, d, vb, va).wait_recv()
        finish(partner(me, d, n), d)

    for d in peers:
        small(1, d, stat_mine, stat_all, partner(me, d, n)).wait_recv()
    total = jnp.sum(stat_all[...], axis=0)
    scale = 1.0 / float(NR * NT * NP)
    stat_out[0, 0] = jnp.sum(total[0:8, :]) * scale
    stat_out[0, 1] = jnp.sum(total[8:16, :]) * scale

    for d in peers:
        back(V, d, vb, va).wait_send()
        small(0, d, dmine, dall, me).wait_send()
        small(1, d, stat_mine, stat_all, me).wait_send()
    before.wait()
    for k, j in [(0, me)] + [(d, partner(me, d, n)) for d in peers]:
        pltpu.make_async_copy(
            prev.at[:, tees(j), :], last_out.at[:, tees(j), :], out_sem.at[1 + k]
        ).wait()


def fused_shards(
    packet_prev, packet_now, potential, kin_rho, kin_theta, kin_phi, damping, inertia, tilt
):
    n = lax.axis_size("slab")
    _, rows, nt, width = packet_now.shape
    cols, full = nt // n, n * rows
    slab = pltpu.VMEM((rows, nt, width), jnp.float32)
    turned = pltpu.VMEM((full, cols, width), jnp.float32)
    pieces = (cols // 8) * (width // 128)
    flat = pltpu.VMEM((pieces, full, 1024), jnp.float32)

    def half(order):
        return [pltpu.VMEM((order, order), jnp.bfloat16)] * 2

    hbm = pl.BlockSpec(memory_space=pltpu.HBM)
    place = pl.BlockSpec(memory_space=pl.ANY)
    smem = pl.BlockSpec(memory_space=pltpu.SMEM)
    dma = pltpu.SemaphoreType.DMA
    field = jax.ShapeDtypeStruct((rows, nt, width), jnp.float32)
    last, before, stats = pl.pallas_call(
        functools.partial(fused, n),
        out_shape=(field, field, jax.ShapeDtypeStruct((1, 2), jnp.float32)),
        in_specs=[hbm] * 9,
        out_specs=(place, place, smem),
        scratch_shapes=[
            slab, slab, slab, slab, turned, slab, turned, turned, slab, turned, slab,
            slab, flat, flat, pltpu.VMEM((nt, 128), jnp.float32),
            *[pltpu.VMEM((order, order), jnp.float32) for order in (full, nt, width)],
            *[pltpu.SMEM((count,), jnp.float32) for count in (rows, rows, nt)],
            *half(full), *half(nt), *half(width),
            pltpu.VMEM((rows, 128), jnp.float32),
            pltpu.VMEM((n, rows, 128), jnp.float32),
            pltpu.VMEM((16, 128), jnp.float32),
            pltpu.VMEM((n, 16, 128), jnp.float32),
            dma((9,)), dma((n + 1,)), dma((4,)), dma((2,)), dma((2,)),
            dma((4, n)), dma((4, n)), dma((2, n)), dma((2, n)),
        ],
        compiler_params=pltpu.CompilerParams(
            collective_id=0, has_side_effects=True, vmem_limit_bytes=60 * 2**20
        ),
        name="chebyshev",
    )(
        packet_now[0], packet_prev[0], potential, kin_rho, kin_theta, kin_phi, damping, inertia,
        tilt,
    )
    return last[None], before[None], stats.T


def fits_fused(mesh):
    n = mesh.shape["slab"]
    return (
        mesh.shape["ka"] == 2
        and STEPS == 2
        and n > 1
        and n & (n - 1) == 0
        and NR == 8 * n
        and NT % (8 * n) == 0
        and NP % 128 == 0
    )


def solution(mesh):
    return jax.shard_map(
        fused_shards if fits_fused(mesh) else shards,
        mesh=mesh,
        in_specs=(
            P("ka", "slab", None, None),
            P("ka", "slab", None, None),
            P("slab", None, None),
            P(),
            P(),
            P(),
            P("slab"),
            P("slab"),
            P(),
        ),
        out_specs=(P("ka", "slab", None, None), P("ka", "slab", None, None), P(None, "ka")),
        check_vma=False,
    )
```

```python
import functools

import jax
import jax.numpy as jnp
from jax import lax
from jax.experimental import pallas as pl
from jax.experimental.pallas import tpu as pltpu
from jax.sharding import PartitionSpec as P

NR = 128
NT = 256
NP = 384
STEPS = 2
JTOT = 60
K_FIRST = 0


HI = lax.Precision.HIGHEST


def padded(cells, sides, width):
    for axis, dim in sides:
        count = lax.axis_size(axis)
        ends = count - 1
        head = lax.slice_in_dim(cells, 0, width, axis=dim)
        tail = lax.slice_in_dim(cells, cells.shape[dim] - width, cells.shape[dim], axis=dim)
        cells = jnp.concatenate(
            [
                lax.ppermute(tail, axis, [(i, (i + 1) % count) for i in range(ends)]),
                cells,
                lax.ppermute(head, axis, [((i + 1) % count, i) for i in range(ends)]),
            ],
            axis=dim,
        )
    return cells


def rho_apply(kin_rho, whole):
    return jnp.einsum("sr,rtp->stp", kin_rho, whole, precision=HI)


def apply_h(q, potential, kin_rho, kin_theta, kin_phi, inertia, tilt):
    kval = (K_FIRST + lax.axis_index("ka")).astype(jnp.float32)
    jj = float(JTOT * (JTOT + 1))
    cent = (jj - 2.0 * kval * kval) / float(JTOT * JTOT)
    lam_here = jnp.sqrt(jj - kval * (kval + 1.0)) / float(JTOT)
    lam_below = jnp.sqrt(jj - (kval - 1.0) * kval) / float(JTOT)
    near = padded(q, (("ka", 0),), 1)
    field = q[0]
    term = rho_apply(
        kin_rho, lax.all_to_all(field, "slab", split_axis=1, concat_axis=0, tiled=True)
    )
    rho_part = lax.all_to_all(term, "slab", split_axis=0, concat_axis=1, tiled=True)
    theta_part = jnp.einsum("ts,rsp->rtp", kin_theta, field, precision=HI)
    rows = field.shape[0] * field.shape[1]
    phi_part = jnp.dot(field.reshape(rows, field.shape[2]), kin_phi, precision=HI).reshape(
        field.shape
    )
    coupling = (
        inertia[:, None, None] * tilt[None, :, None] * (lam_here * near[2] + lam_below * near[0])
    )
    diag = potential + inertia[:, None, None] * cent
    total = rho_part + theta_part + phi_part + diag * field + coupling
    return total[None]


def shards(packet_prev, packet_now, potential, kin_rho, kin_theta, kin_phi, damping, inertia, tilt):
    damp = damping[None, :, None, None]
    cells = float(NR * NT * NP)
    q_prev = packet_prev
    q = packet_now
    partials = []
    for step in range(STEPS):
        image = apply_h(q, potential, kin_rho, kin_theta, kin_phi, inertia, tilt)
        q_new = damp * (2.0 * image - damp * q_prev)
        local_sum = jnp.sum(packet_now * q_new, axis=(1, 2, 3))
        partials.append(lax.psum(local_sum, "slab") / cells)
        q_prev = q
        q = q_new
    intersections = jnp.stack(partials, axis=0)
    return (q, q_prev, intersections)


MESH = pl.DeviceIdType.MESH
Q0, P1, U, V = range(4)


def split(x):
    high = x.astype(jnp.bfloat16)
    return high, (x - high.astype(jnp.float32)).astype(jnp.bfloat16)


def dot3(a, b):
    dot = functools.partial(jnp.dot, preferred_element_type=jnp.float32)
    return dot(a[0], b[0]) + (dot(a[0], b[1]) + dot(a[1], b[0]))


def partner(me, d, n):
    out = 0
    bit = 1
    while bit < n:
        out = out + ((me // bit + d // bit) % 2) * bit
        bit *= 2
    return out


def fused(
    n, q_in, prev_in, pot_in, rho_in, theta_in, phi_in, damp_in, inertia_in, tilt_in,
    last_out, before_out, stat_out,
    q0, prev, pot, near0, qb, p1, pb, ub, ua, vb, va, near1, qx, ux, slope,
    rho, theta, phi, damp, inertia, tilt,
    rho_hi, rho_lo, theta_hi, theta_lo, phi_hi, phi_lo, dmine, dall, stat_mine, stat_all,
    load_sem, out_sem, own_sem, ka_send, ka_recv, send, recv, small_send, small_recv,
):
    rows, nt, width = q0.shape
    cols = qb.shape[1]
    me = lax.axis_index("slab")
    ka = lax.axis_index("ka")
    half = n // 2
    peers = [half]
    for d in range(1, half):
        peers += [d, half + d]

    loads = [
        pltpu.make_async_copy(q_in, q0, load_sem.at[0]),
        pltpu.make_async_copy(prev_in, prev, load_sem.at[1]),
        pltpu.make_async_copy(pot_in, pot, load_sem.at[2]),
        pltpu.make_async_copy(rho_in, rho, load_sem.at[3]),
        pltpu.make_async_copy(theta_in, theta, load_sem.at[4]),
        pltpu.make_async_copy(phi_in, phi, load_sem.at[5]),
        pltpu.make_async_copy(damp_in, damp, load_sem.at[6]),
        pltpu.make_async_copy(inertia_in, inertia, load_sem.at[7]),
        pltpu.make_async_copy(tilt_in, tilt, load_sem.at[8]),
    ]
    for load in loads:
        load.start()

    barrier = pltpu.get_barrier_semaphore()
    for d in peers:
        pl.semaphore_signal(
            barrier, inc=1, device_id={"slab": partner(me, d, n)}, device_id_type=MESH
        )
    pl.semaphore_signal(barrier, inc=1, device_id={"ka": 1 - ka}, device_id_type=MESH)
    pl.semaphore_wait(barrier, n)

    def tees(j):
        return pl.ds(pl.multiple_of(j * cols, cols), cols)

    def rhos(j):
        return pl.ds(pl.multiple_of(j * rows, rows), rows)

    def away(phase, d, src, dst):
        there = partner(me, d, n)
        return pltpu.make_async_remote_copy(
            src_ref=src.at[:, tees(there), :],
            dst_ref=dst.at[rhos(me)],
            send_sem=send.at[phase, d],
            recv_sem=recv.at[phase, d],
            device_id={"slab": there},
            device_id_type=MESH,
        )

    def away_arrival(phase, d, src, dst):
        there = partner(me, d, n)
        return pltpu.make_async_remote_copy(
            src_ref=src.at[:, tees(there), :],
            dst_ref=dst.at[rhos(there)],
            send_sem=send.at[phase, d],
            recv_sem=recv.at[phase, d],
            device_id={"slab": there},
            device_id_type=MESH,
        )

    def back(phase, d, src, dst):
        there = partner(me, d, n)
        return pltpu.make_async_remote_copy(
            src_ref=src.at[rhos(there)],
            dst_ref=dst.at[:, tees(me), :],
            send_sem=send.at[phase, d],
            recv_sem=recv.at[phase, d],
            device_id={"slab": there},
            device_id_type=MESH,
        )

    def back_arrival(phase, d, src, dst):
        there = partner(me, d, n)
        return pltpu.make_async_remote_copy(
            src_ref=src.at[rhos(there)],
            dst_ref=dst.at[:, tees(there), :],
            send_sem=send.at[phase, d],
            recv_sem=recv.at[phase, d],
            device_id={"slab": there},
            device_id_type=MESH,
        )

    def across(k, src, dst):
        return pltpu.make_async_remote_copy(
            src_ref=src,
            dst_ref=dst,
            send_sem=ka_send.at[k],
            recv_sem=ka_recv.at[k],
            device_id={"ka": 1 - ka},
            device_id_type=MESH,
        )

    def small(k, d, src, dst, slot):
        there = partner(me, d, n)
        return pltpu.make_async_remote_copy(
            src_ref=src,
            dst_ref=dst.at[slot],
            send_sem=small_send.at[k, d],
            recv_sem=small_recv.at[k, d],
            device_id={"slab": there},
            device_id_type=MESH,
        )

    across(0, q_in, near0).start()
    for d in peers:
        away(Q0, d, q_in, qb).start()
    own_q = pltpu.make_async_copy(q_in.at[:, tees(me), :], qb.at[rhos(me)], own_sem.at[Q0])
    own_q.start()

    for load in loads:
        load.wait()
    for r in range(rows):
        dmine[r : r + 1, :] = jnp.full((1, dmine.shape[1]), damp[r], jnp.float32)
    for d in peers:
        small(0, d, dmine, dall, me).start()
    dall[me] = dmine[...]

    @pl.loop(0, nt // 8)
    def _(i):
        at = pl.ds(pl.multiple_of(8 * i, 8), 8)
        slope[at, :] = jnp.concatenate(
            [jnp.full((1, 128), tilt[8 * i + k], jnp.float32) for k in range(8)], axis=0
        )

    for ref, high, low in (
        (rho, rho_hi, rho_lo), (theta, theta_hi, theta_lo), (phi, phi_hi, phi_lo)
    ):
        high[...], low[...] = split(ref[...])

    kval = (K_FIRST + ka).astype(jnp.float32)
    kmin = float(K_FIRST)
    jj = float(JTOT * (JTOT + 1))
    cent = (jj - 2.0 * kval * kval) / float(JTOT * JTOT)
    lam = ((jj - kmin * (kmin + 1.0)) ** 0.5) / float(JTOT)

    def image(field, near, r):
        x = field[r]
        parts = split(x)
        total = dot3((theta_hi[...], theta_lo[...]), parts)
        total += dot3(parts, (phi_hi[...], phi_lo[...]))
        total += (pot[r] + inertia[r] * cent) * x
        tilted = (inertia[r] * lam) * slope[...]
        return total + jnp.concatenate([tilted] * (width // 128), axis=1) * near[r]

    across(0, q_in, near0).wait()

    @pl.loop(0, rows)
    def _(r):
        p1[r] = damp[r] * (2.0 * image(q0, near0, r) - damp[r] * prev[r])

    for d in peers:
        away(Q0, d, q_in, qb).wait_send()
        away(P1, d, p1, pb).start()
    own_p = pltpu.make_async_copy(p1.at[:, tees(me), :], pb.at[rhos(me)], own_sem.at[P1])
    own_p.start()
    for d in peers:
        away_arrival(Q0, d, q_in, qb).wait_recv()
    own_q.wait()

    chunks = [(b, c) for b in range(cols // 8) for c in range(width // 128)]
    full = n * rows

    def wide(ref, b, c):
        return ref[:, 8 * b : 8 * b + 8, 128 * c : 128 * c + 128].reshape(full, 1024)

    def narrow(ref, b, c, value):
        ref[:, 8 * b : 8 * b + 8, 128 * c : 128 * c + 128] = value.reshape(full, 8, 128)

    for i, (b, c) in enumerate(chunks):
        x = wide(qb, b, c)
        qx[i] = x
        u = dot3((rho_hi[...], rho_lo[...]), split(x))
        ux[i] = u
        narrow(ub, b, c, u)

    for d in peers:
        away(P1, d, p1, pb).wait_send()
        back(U, d, ub, ua).start()
    own_u = pltpu.make_async_copy(ub.at[rhos(me)], ua.at[:, tees(me), :], own_sem.at[U])
    own_u.start()
    for d in peers:
        away_arrival(P1, d, p1, pb).wait_recv()
        small(0, d, dmine, dall, partner(me, d, n)).wait_recv()
    own_p.wait()

    dcol = 2.0 * dall[...].reshape(full, 128)
    dwide = jnp.concatenate([dcol] * 8, axis=1)
    acc2 = jnp.zeros((8, 128), jnp.float32)
    for i, (b, c) in enumerate(chunks):
        x = wide(pb, b, c) + dwide * ux[i]
        v = dot3((rho_hi[...], rho_lo[...]), split(x))
        narrow(vb, b, c, v)
        prod = (qx[i] * v) * dwide
        part = jnp.sum(prod.reshape(full // 8, 8, 1024), axis=0)
        for k in range(8):
            acc2 += part[:, 128 * k : 128 * k + 128]
    stat_mine[8:16, :] = acc2

    for d in peers:
        back(U, d, ub, ua).wait_send()
        back(V, d, vb, va).start()
    own_v = pltpu.make_async_copy(vb.at[rhos(me)], va.at[:, tees(me), :], own_sem.at[V])
    own_v.start()
    for d in peers:
        back_arrival(U, d, ub, ua).wait_recv()
    own_u.wait()

    def gather(prod):
        part = jnp.sum(prod.reshape(nt // 8, 8, width), axis=0)
        out = part[:, :128]
        for k in range(1, width // 128):
            out += part[:, 128 * k : 128 * k + 128]
        return out

    stat_mine[0:8, :] = jnp.zeros((8, 128), jnp.float32)

    @pl.loop(0, rows)
    def _(r):
        new = p1[r] + (2.0 * damp[r]) * ua[r]
        p1[r] = new
        stat_mine[0:8, :] += gather(q0[r] * new)

    across(1, p1, near1).start()
    before = pltpu.make_async_copy(p1, before_out, out_sem.at[0])
    before.start()
    across(1, p1, near1).wait()

    @pl.loop(0, rows)
    def _(r):
        new = damp[r] * (2.0 * image(p1, near1, r) - damp[r] * q0[r])
        prev[r] = new
        stat_mine[8:16, :] += gather(q0[r] * new)

    for d in peers:
        small(1, d, stat_mine, stat_all, me).start()
    stat_all[me] = stat_mine[...]

    def finish(j, k):
        for r in range(rows):
            prev[r, tees(j), :] += (2.0 * damp[r]) * va[r, tees(j), :]
        pltpu.make_async_copy(
            prev.at[:, tees(j), :], last_out.at[:, tees(j), :], out_sem.at[1 + k]
        ).start()

    own_v.wait()
    finish(me, 0)
    for d in peers:
        back_arrival(V, d, vb, va).wait_recv()
        finish(partner(me, d, n), d)

    for d in peers:
        small(1, d, stat_mine, stat_all, partner(me, d, n)).wait_recv()
    total = jnp.sum(stat_all[...], axis=0)
    scale = 1.0 / float(NR * NT * NP)
    stat_out[0, 0] = jnp.sum(total[0:8, :]) * scale
    stat_out[0, 1] = jnp.sum(total[8:16, :]) * scale

    for d in peers:
        back(V, d, vb, va).wait_send()
        small(0, d, dmine, dall, me).wait_send()
        small(1, d, stat_mine, stat_all, me).wait_send()
    before.wait()
    for k, j in [(0, me)] + [(d, partner(me, d, n)) for d in peers]:
        pltpu.make_async_copy(
            prev.at[:, tees(j), :], last_out.at[:, tees(j), :], out_sem.at[1 + k]
        ).wait()


def fused_shards(
    packet_prev, packet_now, potential, kin_rho, kin_theta, kin_phi, damping, inertia, tilt
):
    n = lax.axis_size("slab")
    _, rows, nt, width = packet_now.shape
    cols, full = nt // n, n * rows
    slab = pltpu.VMEM((rows, nt, width), jnp.float32)
    turned = pltpu.VMEM((full, cols, width), jnp.float32)
    pieces = (cols // 8) * (width // 128)
    flat = pltpu.VMEM((pieces, full, 1024), jnp.float32)

    def half(order):
        return [pltpu.VMEM((order, order), jnp.bfloat16)] * 2

    hbm = pl.BlockSpec(memory_space=pltpu.HBM)
    place = pl.BlockSpec(memory_space=pl.ANY)
    smem = pl.BlockSpec(memory_space=pltpu.SMEM)
    dma = pltpu.SemaphoreType.DMA
    field = jax.ShapeDtypeStruct((rows, nt, width), jnp.float32)
    last, before, stats = pl.pallas_call(
        functools.partial(fused, n),
        out_shape=(field, field, jax.ShapeDtypeStruct((1, 2), jnp.float32)),
        in_specs=[hbm] * 9,
        out_specs=(place, place, smem),
        scratch_shapes=[
            slab, slab, slab, slab, turned, slab, turned, turned, slab, turned, slab,
            slab, flat, flat, pltpu.VMEM((nt, 128), jnp.float32),
            *[pltpu.VMEM((order, order), jnp.float32) for order in (full, nt, width)],
            *[pltpu.SMEM((count,), jnp.float32) for count in (rows, rows, nt)],
            *half(full), *half(nt), *half(width),
            pltpu.VMEM((rows, 128), jnp.float32),
            pltpu.VMEM((n, rows, 128), jnp.float32),
            pltpu.VMEM((16, 128), jnp.float32),
            pltpu.VMEM((n, 16, 128), jnp.float32),
            dma((9,)), dma((n + 1,)), dma((4,)), dma((2,)), dma((2,)),
            dma((4, n)), dma((4, n)), dma((2, n)), dma((2, n)),
        ],
        compiler_params=pltpu.CompilerParams(
            collective_id=0, has_side_effects=True, vmem_limit_bytes=60 * 2**20
        ),
        name="chebyshev",
    )(
        packet_now[0], packet_prev[0], potential, kin_rho, kin_theta, kin_phi, damping, inertia,
        tilt,
    )
    return last[None], before[None], stats.T


def fits_fused(mesh):
    n = mesh.shape["slab"]
    return (
        mesh.shape["ka"] == 2
        and STEPS == 2
        and n > 1
        and n & (n - 1) == 0
        and NR == 8 * n
        and NT % (8 * n) == 0
        and NP % 128 == 0
    )


def solution(mesh):
    return jax.shard_map(
        fused_shards if fits_fused(mesh) else shards,
        mesh=mesh,
        in_specs=(
            P("ka", "slab", None, None),
            P("ka", "slab", None, None),
            P("slab", None, None),
            P(),
            P(),
            P(),
            P("slab"),
            P("slab"),
            P(),
        ),
        out_specs=(P("ka", "slab", None, None), P("ka", "slab", None, None), P(None, "ka")),
        check_vma=False,
    )
```
